32 devices in a mesh: table: 4 (over x, core), batch: 8 (over z, y).
Axes of the slice: x: 2, y: 2, z: 4, core: 2. Of those that a mesh axis runs over, the one named last changes fastest.
Arguments:
- emb_table: bfloat16 [16384, 256], P('table'), may hold values from -2 to 2
- feature_ids: int32 [256, 1024, 8], P('batch', 'table'), may hold values from 0 to 4095
- projection: bfloat16 [1024, 256], P('table'), may hold values from -0.1875 to 0.1875
- norm_gain: float32 [256], replicated, may hold values from 0.1 to 1.9
- gate_weight: bfloat16 [256, 512], replicated, may hold values from -0.375 to 0.375
- up_weight: bfloat16 [256, 512], replicated, may hold values from -0.375 to 0.375
- down_weight: bfloat16 [512, 256], replicated, may hold values from -0.25 to 0.25
- out_grad: bfloat16 [256, 1024, 256], P(('batch', 'table')), may hold values from -12 to 12
Outputs:
- block_out: bfloat16 [256, 1024, 256], P(('batch', 'table'))
- table_grad: float32 [16384, 256], P(('table', 'batch'))
- projection_grad: float32 [1024, 256], P('table')
- gain_grad: float32 [256], replicated
- gate_grad: float32 [256, 512], replicated
- up_grad: float32 [256, 512], replicated
- down_grad: float32 [512, 256], replicated
The draws below stay inside these ranges and needn't reach their ends.
Inputs may be any that keep to these rules, and one draw needn't show every extreme that they name: `feature_ids`: an id names a row of the table shard of the device that holds the feature's table.
All inputs are finite; a program needn't handle non-finite values.
Results may differ from the reference program's by a relative error of at most 0.035.
Values may be sent and summed in bfloat16 or wider, within the bound.
A program may use at most 192 MiB of HBM per device.

```python
import math
import jax
import jax.numpy as jnp
import numpy as np
from jax import lax

D = 256
K = 256
F = 1024
H = 512
POOL = 8
ROWS_DEV = 4096
SAMP = 32
SAMPLES = 256
ROWS = 16384
N_TABLE = 4


def plant(values, rng, least, high):
    index_at = [jax.random.randint(jax.random.fold_in(rng, axis), (), 0, length) for axis, length in enumerate(values.shape)]
    longest = values.shape.index(max(values.shape))
    beside = index_at[:longest] + [(index_at[longest] + 1) % values.shape[longest]] + index_at[longest + 1:]
    return values.at[tuple(index_at)].set(least).at[tuple(beside)].set(high)


def strengthened(values, stream_key, source, target, shards_of, factor):
    def block_of(axis_at):
        return (jnp.arange(values.shape[axis_at]) // (values.shape[axis_at] // shards_of)).reshape((-1,) + (1,) * (values.ndim - 1 - axis_at))

    near = jax.random.permutation(stream_key, shards_of)[block_of(target)]
    second = (block_of(target) + shards_of // 2) % shards_of
    return jnp.where((block_of(source) == near) | (block_of(source) == second), factor * values, values)


def levels(own_key, extent, cuts, low, largest):
    factor_of = 1.0
    for axis_at, parts in cuts:
        heights = jax.random.uniform(jax.random.fold_in(jax.random.fold_in(own_key, 6), axis_at), (parts,), jnp.float32, low / len(cuts), largest / len(cuts))
        factor_of = factor_of * jnp.repeat(jnp.exp(heights), extent[axis_at] // parts).reshape((-1,) + (1,) * (len(extent) - 1 - axis_at))
    return factor_of


def rank_bounds(number_of, lean):
    loads = [(1 << 20) // math.isqrt(rank ** lean) + 1 for rank in range(1, number_of + 1)]
    scale = 1 + sum(loads) // (1 << 30)
    return np.cumsum(np.array([max(1, weight // scale) for weight in loads]))


def ranked(key, shape, amount, skew):
    table = rank_bounds(amount, skew)
    ticket = jax.random.randint(jax.random.fold_in(key, 1), shape, 0, int(table[amount - 1]))
    standing = jnp.searchsorted(jnp.asarray(table, jnp.int32), ticket, side="right")
    return jax.random.permutation(jax.random.fold_in(key, 2), amount)[standing].astype(jnp.int32)


def gaussian(own_key, extent, scale, most, cuts=(), held_as=jnp.bfloat16):
    array = scale * jax.random.normal(own_key, extent, jnp.float32)
    if cuts:
        array = array * levels(own_key, extent, cuts, -0.22, 0.18)
    return jnp.clip(array, -most, most).astype(held_as)


def noise_with(stream_key, extent, deviation, limit, cuts, heavy, kind=jnp.bfloat16):
    drawn = deviation * jax.random.normal(stream_key, extent, jnp.float32)
    if cuts:
        drawn = drawn * levels(stream_key, extent, cuts, -0.22, 0.18)
    return jnp.clip(strengthened(drawn, jax.random.fold_in(stream_key, 3), *heavy), -limit, limit).astype(kind)


def setup_inputs(seed: int = 0) -> dict:
    key_of = jax.random.split(jax.random.key(seed), 9)
    emb_table = gaussian(key_of[0], (ROWS, D), 0.35, 2.0, ((0, 4),))
    feature_ids = plant(ranked(key_of[1], (SAMPLES, F, POOL), ROWS_DEV, 2), jax.random.fold_in(key_of[1], 3), 0, ROWS_DEV - 1).astype(jnp.int32)
    projection = gaussian(key_of[2], (F, K), F ** -0.5, 0.1875, ((0, 4),))
    norm_gain = jnp.clip(1.0 + 0.18 * jax.random.normal(key_of[3], (K,), jnp.float32), 0.1, 1.9)
    gate_weight = gaussian(key_of[4], (K, H), K ** -0.5, 0.375)
    up_weight = gaussian(key_of[5], (K, H), K ** -0.5, 0.375)
    down_weight = gaussian(key_of[6], (H, D), H ** -0.5, 0.25)
    out_grad = noise_with(key_of[7], (SAMPLES, F, D), 1.0, 12.0, ((0, 32),), (0, 2, 32, 2.75))
    return dict(emb_table=emb_table, feature_ids=feature_ids, projection=projection, norm_gain=norm_gain, gate_weight=gate_weight, up_weight=up_weight, down_weight=down_weight, out_grad=out_grad)


epsilon = 1e-06

def mlp_forward(interact, norm_gain, gate_weight, up_weight, down_weight):
    mean_sq = lax.optimization_barrier(jnp.mean(interact * interact, axis=-1, keepdims=True))
    inv_rms = lax.rsqrt(mean_sq + epsilon)
    normed = interact * inv_rms
    scaled = (normed * norm_gain).astype(jnp.bfloat16)
    gate_pre = jnp.dot(scaled, gate_weight, preferred_element_type=jnp.float32)
    up_pre = jnp.dot(scaled, up_weight, preferred_element_type=jnp.float32)
    hidden = (jax.nn.silu(gate_pre) * up_pre).astype(jnp.bfloat16)
    result = jnp.dot(hidden, down_weight, preferred_element_type=jnp.float32).astype(jnp.bfloat16)
    return (result, (inv_rms, normed, scaled, gate_pre, up_pre, hidden))

def contract(left, right, left_dim, right_dim):
    return lax.dot_general(left, right, (((left_dim,), (right_dim,)), ((), ())), preferred_element_type=jnp.float32)

def mlp_backward(stored, grad_rows, norm_gain, gate_weight, up_weight, down_weight):
    inv_rms, normed, scaled, gate_pre, up_pre, hidden = stored
    hidden_grad = contract(grad_rows, down_weight, 1, 1)
    down_part = contract(hidden, grad_rows, 0, 0)
    sigmoid_gate = jax.nn.sigmoid(gate_pre)
    up_pre_grad = (hidden_grad * jax.nn.silu(gate_pre)).astype(jnp.bfloat16)
    gate_pre_grad = (hidden_grad * up_pre * sigmoid_gate * (1.0 + gate_pre * (1.0 - sigmoid_gate))).astype(jnp.bfloat16)
    gate_part = contract(scaled, gate_pre_grad, 0, 0)
    up_part = contract(scaled, up_pre_grad, 0, 0)
    scaled_grad = contract(gate_pre_grad, gate_weight, 1, 1) + contract(up_pre_grad, up_weight, 1, 1)
    gain_part = lax.optimization_barrier(jnp.sum(scaled_grad * normed, axis=0))
    inner_term = scaled_grad * norm_gain
    interact_grad = inv_rms * (inner_term - normed * lax.optimization_barrier(jnp.mean(inner_term * normed, axis=-1, keepdims=True)))
    return (interact_grad.astype(jnp.bfloat16), gate_part, up_part, down_part, gain_part)

def round_partial(values):
    return lax.optimization_barrier(values.astype(jnp.bfloat16)).astype(jnp.float32)

def reference(emb_table, feature_ids, projection, norm_gain, gate_weight, up_weight, down_weight, out_grad):
    shards = N_TABLE
    feat_here = F // N_TABLE
    blocks = SAMPLES // SAMP
    offsets = jnp.arange(F, dtype=jnp.int32) // feat_here * ROWS_DEV
    ids_blocks = feature_ids.reshape(blocks, SAMP, F, POOL)
    grad_blocks = out_grad.reshape(blocks, SAMP, F, D)
    proj_wide = projection.astype(jnp.float32)
    proj_shards = proj_wide.reshape(shards, feat_here, K)
    totals = (jnp.zeros((ROWS, D), jnp.float32), jnp.zeros((F, K), jnp.float32), jnp.zeros((K, H), jnp.float32), jnp.zeros((K, H), jnp.float32), jnp.zeros((H, D), jnp.float32), jnp.zeros((K,), jnp.float32))

    def block_step(sums, inputs):
        block_ids, block_grad = inputs
        row_ids = (block_ids + offsets[None, :, None]).astype(jnp.int32)
        embeds = lax.optimization_barrier(jnp.sum(emb_table[row_ids].astype(jnp.float32), axis=2)).astype(jnp.bfloat16)
        embeds_wide = embeds.astype(jnp.float32)
        emb_shards = embeds_wide.reshape(SAMP, shards, feat_here, D)
        z_partial = round_partial(jnp.einsum('stfd,tfk->stdk', emb_shards, proj_shards))
        inter_map = lax.optimization_barrier(jnp.sum(z_partial, axis=1)).astype(jnp.bfloat16)
        inter_wide = inter_map.astype(jnp.float32)
        interact = jnp.einsum('sfd,sdk->sfk', embeds_wide, inter_wide)
        result, stored = mlp_forward(interact.reshape(SAMP * F, K), norm_gain, gate_weight, up_weight, down_weight)
        interact_grad, gate_part, up_part, down_part, gain_part = mlp_backward(stored, block_grad.reshape(SAMP * F, D), norm_gain, gate_weight, up_weight, down_weight)
        igrad_wide = interact_grad.astype(jnp.float32).reshape(SAMP, F, K)
        zgrad_partial = round_partial(jnp.einsum('stfd,stfk->stdk', emb_shards, igrad_wide.reshape(SAMP, shards, feat_here, K)))
        inter_grad = lax.optimization_barrier(jnp.sum(zgrad_partial, axis=1)).astype(jnp.bfloat16)
        igrad_map = inter_grad.astype(jnp.float32)
        embed_grad = (jnp.einsum('sfk,sdk->sfd', igrad_wide, inter_wide) + jnp.einsum('fk,sdk->sfd', proj_wide, igrad_map)).astype(jnp.bfloat16)
        spread = jnp.broadcast_to(embed_grad.astype(jnp.float32)[:, :, None, :], (SAMP, F, POOL, D))
        table_sum = sums[0] + jax.ops.segment_sum(spread.reshape(-1, D), row_ids.reshape(-1), num_segments=ROWS)
        proj_sum = sums[1] + jnp.einsum('sfd,sdk->fk', embeds_wide, igrad_map)
        updated = (table_sum, proj_sum, sums[2] + gate_part, sums[3] + up_part, sums[4] + down_part, sums[5] + gain_part)
        return (updated, result.reshape(SAMP, F, D))
    sums, outputs = lax.scan(block_step, totals, (ids_blocks, grad_blocks))
    block_out = outputs.reshape(SAMPLES, F, D)
    return (block_out, sums[0], sums[1], sums[5], sums[2], sums[3], sums[4])
```

```python
import functools

import jax
import jax.numpy as jnp
import numpy as np
from jax import lax
from jax.experimental import pallas as pl
from jax.experimental.pallas import tpu as pltpu
from jax.sharding import PartitionSpec as P

epsilon = 1e-06
LANES = 128
DIGITS = 8
VMEM_LIMIT = 56 * 1024 * 1024


def contract(left, right, left_dim, right_dim):
    return lax.dot_general(
        left, right, (((left_dim,), (right_dim,)), ((), ())), preferred_element_type=jnp.float32
    )


def row_scale(rows):
    digit = (np.arange(rows) // LANES) % DIGITS
    digit = np.where(digit == DIGITS - 1, 0, digit)
    return jnp.asarray(2.0 ** (-4.0 * digit), jnp.float32)


def lookup_kernel(ids_ref, table_ref, emb_ref, count_ref):
    tile, pool = ids_ref.shape
    rows = count_ref.shape[1]
    groups = rows // (LANES * DIGITS)
    sub = 8
    for start in range(0, tile, sub):
        ids = ids_ref[pl.ds(start, sub), :]
        lane = lax.broadcasted_iota(jnp.int32, (sub, LANES), 1)
        hi = lax.shift_right_logical(ids, 7)
        value = lax.shift_left(jnp.ones_like(ids), 4 * (hi & 7))
        key = (ids & 127) | (lax.shift_right_logical(hi, 3) << 7)
        acc = [jnp.zeros((sub, LANES), jnp.int32) for _ in range(groups)]
        for p in range(pool):
            key_p = jnp.broadcast_to(key[:, p : p + 1], (sub, LANES)) - lane
            value_p = jnp.broadcast_to(value[:, p : p + 1], (sub, LANES))
            for g in range(groups):
                acc[g] = acc[g] + jnp.where(key_p == g * LANES, value_p, 0)
        for g in range(groups):
            for digit in range(DIGITS):
                if digit == DIGITS - 1:
                    part = lax.shift_right_logical(acc[g], 4 * digit)
                else:
                    part = acc[g] & (15 << (4 * digit))
                column = (g * DIGITS + digit) * LANES
                count_ref[pl.ds(start, sub), pl.ds(column, LANES)] = part.astype(
                    jnp.float32
                ).astype(jnp.bfloat16)
    emb_ref[...] = jnp.dot(
        count_ref[...], table_ref[...], preferred_element_type=jnp.float32
    ).astype(jnp.bfloat16)


def lookup(ids, table):
    total, pool = ids.shape
    rows, width = table.shape
    tile = min(256, total)
    return pl.pallas_call(
        lookup_kernel,
        grid=(total // tile,),
        in_specs=[
            pl.BlockSpec((tile, pool), lambda i: (i, 0)),
            pl.BlockSpec((rows, width), lambda i: (0, 0)),
        ],
        out_specs=[
            pl.BlockSpec((tile, width), lambda i: (i, 0)),
            pl.BlockSpec((tile, rows), lambda i: (i, 0)),
        ],
        out_shape=[
            jax.ShapeDtypeStruct((total, width), jnp.bfloat16),
            jax.ShapeDtypeStruct((total, rows), jnp.bfloat16),
        ],
        compiler_params=pltpu.CompilerParams(vmem_limit_bytes=VMEM_LIMIT),
        cost_estimate=pl.CostEstimate(
            flops=2 * total * rows * width,
            bytes_accessed=total * rows * 2 + total * width * 2 + rows * width * 2,
            transcendentals=0,
        ),
        name="lookup",
    )(ids, table)


def sample_kernel(shards, me_ref, *refs):
    x_refs = refs[:shards]
    proj_ref, gain_ref, gate_ref, up_ref, down_ref, og_ref = refs[shards : shards + 6]
    out_ref = refs[shards + 6]
    eg_refs = refs[shards + 7 : 2 * shards + 7]
    proj_acc, gate_acc, up_acc, down_acc, gain_acc = refs[2 * shards + 7 : 2 * shards + 12]
    xs, igs, egs = refs[2 * shards + 12 :]
    me = me_ref[0]
    feat_here = x_refs[0].shape[1]
    features = xs.shape[0]

    @pl.when(pl.program_id(0) == 0)
    def _():
        for acc in (proj_acc, gate_acc, up_acc, down_acc, gain_acc):
            acc[...] = jnp.zeros_like(acc)

    for j in range(shards):
        first = pl.multiple_of((me ^ j) * feat_here, feat_here)
        xs[pl.ds(first, feat_here), :] = x_refs[j][0]
    inter = contract(xs[...], proj_ref[...], 0, 0).astype(jnp.bfloat16)
    gain = gain_ref[...]
    block = min(256, features)
    for start in range(0, features, block):
        rows = pl.ds(start, block)
        interact = jnp.dot(xs[rows, :], inter, preferred_element_type=jnp.float32)
        inv_rms = lax.rsqrt(jnp.mean(interact * interact, axis=-1, keepdims=True) + epsilon)
        normed = interact * inv_rms
        scaled = (normed * gain).astype(jnp.bfloat16)
        gate_pre = jnp.dot(scaled, gate_ref[...], preferred_element_type=jnp.float32)
        up_pre = jnp.dot(scaled, up_ref[...], preferred_element_type=jnp.float32)
        sig = jax.nn.sigmoid(gate_pre)
        silu = gate_pre * sig
        hidden = (silu * up_pre).astype(jnp.bfloat16)
        out_ref[0, rows, :] = jnp.dot(
            hidden, down_ref[...], preferred_element_type=jnp.float32
        ).astype(jnp.bfloat16)
        og = og_ref[0, rows, :]
        hidden_grad = contract(og, down_ref[...], 1, 1)
        down_acc[...] += contract(hidden, og, 0, 0)
        up_grad = (hidden_grad * silu).astype(jnp.bfloat16)
        gate_grad = (hidden_grad * up_pre * (sig + silu * (1.0 - sig))).astype(jnp.bfloat16)
        gate_acc[...] += contract(scaled, gate_grad, 0, 0)
        up_acc[...] += contract(scaled, up_grad, 0, 0)
        scaled_grad = contract(gate_grad, gate_ref[...], 1, 1) + contract(
            up_grad, up_ref[...], 1, 1
        )
        prod = scaled_grad * normed
        gain_acc[...] += jnp.sum(prod, axis=0, keepdims=True)
        mean = jnp.mean(prod * gain, axis=-1, keepdims=True)
        igs[rows, :] = (inv_rms * (scaled_grad * gain - normed * mean)).astype(jnp.bfloat16)
    inter_grad = contract(xs[...], igs[...], 0, 0).astype(jnp.bfloat16)
    egs[...] = (
        contract(igs[...], inter, 1, 1) + contract(proj_ref[...], inter_grad, 1, 1)
    ).astype(jnp.bfloat16)
    for j in range(shards):
        first = pl.multiple_of((me ^ j) * feat_here, feat_here)
        eg_refs[j][0] = egs[pl.ds(first, feat_here), :]
    proj_acc[...] += jnp.dot(xs[...], inter_grad, preferred_element_type=jnp.float32)


def samples_step(me, parts, proj, gain, gate, up, down, out_grad):
    shards = len(parts)
    owned, feat_here, width = parts[0].shape
    features, rank = proj.shape
    hidden = gate.shape[1]
    whole = lambda s, m: (0, 0)
    per_sample = lambda s, m: (s, 0, 0)
    part_spec = pl.BlockSpec((1, feat_here, width), per_sample)
    sums = [(features, rank), (rank, hidden), (rank, hidden), (hidden, width), (1, rank)]
    rows = owned * features
    return pl.pallas_call(
        functools.partial(sample_kernel, shards),
        grid_spec=pltpu.PrefetchScalarGridSpec(
            num_scalar_prefetch=1,
            grid=(owned,),
            in_specs=[part_spec] * shards
            + [
                pl.BlockSpec((features, rank), whole),
                pl.BlockSpec((1, rank), whole),
                pl.BlockSpec((rank, hidden), whole),
                pl.BlockSpec((rank, hidden), whole),
                pl.BlockSpec((hidden, width), whole),
                pl.BlockSpec((1, features, width), per_sample),
            ],
            out_specs=[pl.BlockSpec((1, features, width), per_sample)]
            + [part_spec] * shards
            + [pl.BlockSpec(shape, whole) for shape in sums],
            scratch_shapes=[
                pltpu.VMEM((features, width), jnp.bfloat16),
                pltpu.VMEM((features, rank), jnp.bfloat16),
                pltpu.VMEM((features, width), jnp.bfloat16),
            ],
        ),
        out_shape=[jax.ShapeDtypeStruct((owned, features, width), jnp.bfloat16)]
        + [jax.ShapeDtypeStruct((owned, feat_here, width), jnp.bfloat16)] * shards
        + [jax.ShapeDtypeStruct(shape, jnp.float32) for shape in sums],
        compiler_params=pltpu.CompilerParams(vmem_limit_bytes=VMEM_LIMIT),
        cost_estimate=pl.CostEstimate(
            flops=2 * rows * rank * (9 * hidden + 6 * width),
            bytes_accessed=rows * width * 8,
            transcendentals=rows * hidden,
        ),
        name="samples",
    )(me, *parts, proj, gain, gate, up, down, out_grad)


def scatter_kernel(shards, *refs):
    eg_refs, count_refs = refs[:shards], refs[shards : 2 * shards]
    scale_ref, out_ref = refs[2 * shards :]
    total = contract(eg_refs[0][...], count_refs[0][...], 0, 0)
    for j in range(1, shards):
        total = total + contract(eg_refs[j][...], count_refs[j][...], 0, 0)
    out_ref[...] = (total * scale_ref[...]).T.astype(jnp.bfloat16)


def scatter(grads, counts, scale):
    shards = len(grads)
    total, width = grads[0].shape
    rows = counts[0].shape[1]
    block = min(512, rows)
    return pl.pallas_call(
        functools.partial(scatter_kernel, shards),
        grid=(rows // block,),
        in_specs=[pl.BlockSpec((total, width), lambda i: (0, 0))] * shards
        + [pl.BlockSpec((total, block), lambda i: (0, i))] * shards
        + [pl.BlockSpec((1, block), lambda i: (0, i))],
        out_specs=pl.BlockSpec((block, width), lambda i: (i, 0)),
        out_shape=jax.ShapeDtypeStruct((rows, width), jnp.bfloat16),
        compiler_params=pltpu.CompilerParams(vmem_limit_bytes=VMEM_LIMIT),
        cost_estimate=pl.CostEstimate(
            flops=2 * shards * total * rows * width,
            bytes_accessed=shards * total * (rows + width) * 2,
            transcendentals=0,
        ),
        name="scatter",
    )(*grads, *counts, scale)


def per_device(
    shards,
    emb_table,
    feature_ids,
    projection,
    norm_gain,
    gate_weight,
    up_weight,
    down_weight,
    out_grad,
):
    samples_here, feat_here, pool_size = feature_ids.shape
    rows_here, width = emb_table.shape
    owned = samples_here // shards
    me = lax.axis_index("table")
    scale = row_scale(rows_here)
    table = (emb_table.astype(jnp.float32) * scale[:, None]).astype(jnp.bfloat16)
    proj = lax.all_gather(projection, "table", axis=0, tiled=True)

    swap = lambda value, j: lax.ppermute(value, "table", [(i, i ^ j) for i in range(shards)])
    parts, counts = [None] * shards, [None] * shards
    for j in reversed(range(shards)):
        ids = lax.dynamic_slice_in_dim(feature_ids, (me ^ j) * owned, owned, 0)
        embeds, counts[j] = lookup(ids.reshape(-1, pool_size), table)
        embeds = embeds.reshape(owned, feat_here, width)
        parts[j] = embeds if j == 0 else swap(embeds, j)
    results = samples_step(
        me[None].astype(jnp.int32),
        parts,
        proj,
        norm_gain[None, :],
        gate_weight,
        up_weight,
        down_weight,
        out_grad,
    )
    block_out = results[0]
    grads = [
        (g if j == 0 else swap(g, j)).reshape(-1, width)
        for j, g in enumerate(results[1 : shards + 1])
    ]
    proj_part, gate_part, up_part, down_part, gain_part = results[shards + 1 :]
    table_term = scatter(grads, counts, scale[None, :])
    table_grad = lax.psum_scatter(
        table_term, "batch", scatter_dimension=0, tiled=True
    ).astype(jnp.float32)
    proj_own = lax.psum_scatter(
        proj_part.astype(jnp.bfloat16), "table", scatter_dimension=0, tiled=True
    )
    projection_grad = lax.psum(proj_own, "batch").astype(jnp.float32)
    gate_grad, up_grad, down_grad, gain_grad = lax.psum(
        (gate_part, up_part, down_part, gain_part), ("table", "batch")
    )
    return (
        block_out,
        table_grad,
        projection_grad,
        gain_grad[0],
        gate_grad,
        up_grad,
        down_grad,
    )


def solution(mesh):
    shards = mesh.shape["table"]
    return jax.shard_map(
        functools.partial(per_device, shards),
        mesh=mesh,
        in_specs=(
            P("table", None),
            P("batch", "table", None),
            P("table", None),
            P(),
            P(),
            P(),
            P(),
            P(("batch", "table"), None, None),
        ),
        out_specs=(
            P(("batch", "table"), None, None),
            P(("table", "batch"), None),
            P("table", None),
            P(),
            P(),
            P(),
            P(),
        ),
        check_vma=False,
    )
```
